32 devices in a mesh: dp: 4 (over z), expert: 8 (over y, x, core).
Axes of the slice: x: 2, y: 2, z: 4, core: 2. Of those that a mesh axis runs over, the one named last changes fastest.
Arguments:
- tokens: bfloat16 [4096, 2048], P(('dp', 'expert')), may hold values from -6 to 6
- expert_ids: int32 [4096, 6], P(('dp', 'expert')), may hold values from 0 to 15, all different within a row; in each aligned block of 128 rows (0 to 127, 128 to 255, ...) at most 64 rows name the same one
- combine_weight: float32 [4096, 6], P(('dp', 'expert')), may hold values from 0.05 to 1
- partner: int32 [8], replicated, may hold values from 0 to 7, as said below
- w_up: bfloat16 [2048, 16, 768], P(None, 'expert'), may hold values from -0.125 to 0.125
- w_down: bfloat16 [2048, 16, 768], P(None, 'expert'), may hold values from -0.21875 to 0.21875
- out_grad: bfloat16 [4096, 2048], P(('dp', 'expert')), may hold values from -6 to 6
Outputs:
- output: bfloat16 [4096, 2048], P(('dp', 'expert'))
- input_grad: bfloat16 [4096, 2048], P(('dp', 'expert'))
- grad_up: bfloat16 [2048, 16, 768], P('dp', 'expert')
- grad_down: bfloat16 [2048, 16, 768], P('dp', 'expert')
The draws below stay inside these ranges and needn't reach their ends.
Inputs may be any that keep to these rules, and one draw needn't show every extreme that they name: `expert_ids`: each token names 6 different experts; among the tokens of one device (aligned blocks of 128 tokens) no expert is named more than 64 times, and in some blocks one is named exactly 64 times. partner[partner[j]] = j and partner[j] != j for every j.
All inputs are finite; a program needn't handle non-finite values.
Results may differ from the reference program's by a relative error of at most 0.017.
Values may be sent and summed in bfloat16 or wider, within the bound.
No kernel may reach another device: no remote copies, remote signals or barrier semaphores. Data moves between devices by JAX's collectives and lax.ppermute only.
A program may use at most 192 MiB of HBM per device.

```python
import math
import jax
import jax.numpy as jnp
import numpy as np
from jax import lax

D = 2048
H = 768
TOPK = 6
EXP_DEV = 2
TOK_DEV = 128
OWNERS = 8
DP_GROUPS = 4
EXPERTS = 16
TOKENS = 4096
CAP = 64


def draw_partner(key, part):
    order = jax.random.permutation(key, OWNERS).astype(jnp.int32)
    paired = order.reshape(OWNERS // 2, 2)[:, ::-1].reshape(OWNERS)
    return jnp.zeros((OWNERS,), jnp.int32).at[order].set(paired)


def strengthened(values, own_key, source, target, shards_of, factor):
    def block_of(axis_at):
        return (jnp.arange(values.shape[axis_at]) // (values.shape[axis_at] // shards_of)).reshape((-1,) + (1,) * (values.ndim - 1 - axis_at))

    first = jax.random.permutation(own_key, shards_of)[block_of(target)]
    other_side = (block_of(target) + shards_of // 2) % shards_of
    return jnp.where((block_of(source) == first) | (block_of(source) == other_side), factor * values, values)


def levels(stream_key, shape, shards, least, top_value):
    level, own = 1.0, jax.random.fold_in(stream_key, 6)
    for dim, shards_of in shards:
        steps = jnp.exp(jax.random.uniform(jax.random.fold_in(own, dim), (shards_of,), jnp.float32, least / len(shards), top_value / len(shards)))
        level = level * jnp.repeat(steps, shape[dim] // shards_of).reshape([-1 if axis == dim else 1 for axis in range(len(shape))])
    return level


def shared_out(rng, own, number, rows, number_of, top, bound, lean):
    sequence = jax.random.permutation(rng, number_of)
    crowded, usual = load_shares(number_of, rows * top, bound, lean, True), load_shares(number_of, rows * top, bound, lean, False)
    places = jnp.arange(number_of)

    def named(sizes, rotation):
        used = int((sizes > 0).sum())
        fixed = max(1, used // 4)
        moved = fixed + (places - fixed + rotation * (used - fixed)) % max(1, number_of - fixed)
        return jnp.zeros((number_of,), jnp.int32).at[sequence[jnp.where(places < fixed, places, moved)]].set(jnp.asarray(sizes, jnp.int32))

    sizes = jnp.where(number % 4 == 0, named(crowded, number // 4), named(usual, number - number // 4 - 1))
    mixed = jax.random.permutation(jax.random.fold_in(own, 3), number_of)
    giver, sink = mixed[0:number_of // 2 * 2:2], mixed[1:number_of // 2 * 2:2]
    slack = jnp.minimum(sizes[giver] - 1, bound - sizes[sink]) // 2
    slack = jnp.where((giver == sequence[0]) | (sink == sequence[0]) | (sizes[sink] == 0), 0, jnp.maximum(slack, 0))
    moved = jax.random.randint(jax.random.fold_in(own, 4), (number_of // 2,), 0, 1 << 20) % (slack + 1)
    sizes = sizes.at[giver].add(-moved).at[sink].add(moved)
    items = jnp.searchsorted(jnp.cumsum(sizes), jnp.arange(rows * top), side="right").astype(jnp.int32)
    listing = items.reshape(top, rows).T
    listing = listing[jax.random.permutation(jax.random.fold_in(own, 1), rows)]
    rotation = jax.random.randint(jax.random.fold_in(own, 2), (rows, 1), 0, top)
    return jnp.take_along_axis(listing, (jnp.arange(top)[None, :] + rotation) % top, axis=1)


def load_shares(count, total, reach, slope, full):
    loads = [(1 << 20) // math.isqrt(rank ** slope) + 1 for rank in range(1, count + 1)]
    largest = reach if full else min(reach, max(-(-total // count), total * loads[0] // sum(loads)))
    least = 1 if total - largest >= count - 1 else 0
    counts, spare = [largest] + [least] * (count - 1), total - largest - least * (count - 1)
    while spare > 0:
        movable = [i for i in range(1, count) if counts[i] < largest] or [i for i in range(1, count) if counts[i] < reach]
        mass, left = sum([loads[i] for i in movable]), spare
        for i in movable:
            addition = min(reach - counts[i], max(1, left * loads[i] // mass), spare)
            counts[i] = counts[i] + addition
            spare = spare - addition
    return np.array(counts)


def gaussian(rng, extent, width, bound, cuts=(), held_as=jnp.bfloat16):
    loudness = levels(rng, extent, cuts, -0.22, 0.18) if cuts else 1.0
    entries = jax.random.normal(rng, extent, jnp.float32) * width * loudness
    return jnp.minimum(jnp.maximum(entries, -bound), bound).astype(held_as)


def gaussian_with(key, shape, spread, most, split, heavy, kind=jnp.bfloat16):
    values = spread * jax.random.normal(key, shape, jnp.float32)
    if split:
        values = values * levels(key, shape, split, -0.22, 0.18)
    return jnp.clip(strengthened(values, jax.random.fold_in(key, 3), *heavy), -most, most).astype(kind)


def setup_inputs(seed: int = 0) -> dict:
    key_of = jax.random.split(jax.random.key(seed), 8)
    tokens = gaussian_with(key_of[0], (TOKENS, D), 1.0, 6.0, ((0, 32),), (0, 1, 32, 2.75))
    expert_ids_keys = jax.random.split(jax.random.fold_in(key_of[1], 1), TOKENS // TOK_DEV)
    expert_ids_turns = jax.random.permutation(jax.random.fold_in(key_of[1], 3), TOKENS // TOK_DEV)
    expert_ids = jax.vmap(lambda own, number: shared_out(jax.random.fold_in(key_of[1], 2), own, number, TOK_DEV, EXPERTS, TOPK, CAP, 2))(expert_ids_keys, expert_ids_turns).reshape((TOKENS, TOPK))
    combine_weight = jnp.clip(jnp.exp(math.log(1.0) - 2.9957323 * jax.random.uniform(key_of[2], (TOKENS, TOPK), jnp.float32) ** levels(key_of[2], (TOKENS, TOPK), ((0, 32),), -0.2, 0.2)), 0.05, 1.0)
    partner = draw_partner(jax.random.fold_in(key_of[7], 71), 0)
    w_up = gaussian(key_of[4], (D, EXPERTS, H), D ** -0.5, 0.125, ((1, 8),))
    w_down = gaussian(key_of[5], (D, EXPERTS, H), H ** -0.5, 0.21875, ((1, 8),))
    out_grad = gaussian(key_of[6], (TOKENS, D), 1.0, 6.0, ((0, 32),))
    return dict(tokens=tokens, expert_ids=expert_ids, combine_weight=combine_weight, partner=partner, w_up=w_up, w_down=w_down, out_grad=out_grad)


def silu_slope(hidden_pre):
    sigma = jax.nn.sigmoid(hidden_pre)
    return sigma * (1.0 + hidden_pre * (1.0 - sigma))


def reference(tokens, expert_ids, combine_weight, partner, w_up, w_down, out_grad):
    blocks = DP_GROUPS * OWNERS
    per_block = TOK_DEV * TOPK
    named = expert_ids.reshape(blocks, per_block).astype(jnp.int32)
    onehot = (named[:, :, None] == jnp.arange(EXPERTS, dtype=jnp.int32)[None, None, :]).astype(jnp.int32)
    earlier = jnp.cumsum(onehot, axis=1) - onehot
    position = jnp.sum(earlier * onehot, axis=2).astype(jnp.int32)
    block_index = jnp.arange(blocks, dtype=jnp.int32)[:, None]
    group_index = jnp.broadcast_to(block_index // OWNERS, named.shape).astype(jnp.int32)
    within = jnp.arange(per_block, dtype=jnp.int32)[None, :]
    token_index = (block_index * TOK_DEV + within // TOPK).astype(jnp.int32)
    slot_row = ((block_index % OWNERS) * CAP + position).astype(jnp.int32)
    token_table = jnp.full((EXPERTS, DP_GROUPS, OWNERS * CAP), TOKENS, jnp.int32)
    token_table = token_table.at[named, group_index, slot_row].set(token_index)
    coef_table = jnp.zeros((EXPERTS, DP_GROUPS, OWNERS * CAP), jnp.float32)
    coef_table = coef_table.at[named, group_index, slot_row].set(
        combine_weight.reshape(blocks, per_block).astype(jnp.float32))
    padded_tokens = jnp.concatenate([tokens, jnp.zeros((1, D), tokens.dtype)], axis=0)
    padded_grad = jnp.concatenate([out_grad, jnp.zeros((1, D), out_grad.dtype)], axis=0)
    up_stack = jnp.moveaxis(w_up, 1, 0)
    down_stack = jnp.moveaxis(w_down, 1, 0)
    grad_scale = 1.0 / TOK_DEV
    slot_rows = OWNERS * CAP

    def one_expert(totals, pieces):
        out_total, grad_total = totals
        token_rows, weight, up_mat, down_mat = pieces
        flat_rows = token_rows.reshape(-1)
        weight_col = weight.reshape(-1)[:, None]
        inputs = padded_tokens[flat_rows]
        hidden_pre = jnp.dot(inputs, up_mat, preferred_element_type=jnp.float32)
        activated = jax.nn.silu(hidden_pre).astype(jnp.bfloat16)
        expert_out = jnp.dot(activated, down_mat.T, preferred_element_type=jnp.float32).astype(jnp.bfloat16)
        out_total = out_total.at[flat_rows].add(weight_col * expert_out.astype(jnp.float32), mode="drop")
        grad_out = (weight_col * padded_grad[flat_rows].astype(jnp.float32)).astype(jnp.bfloat16)
        grad_act = jnp.dot(grad_out, down_mat, preferred_element_type=jnp.float32)
        grad_pre = (grad_act * silu_slope(hidden_pre)).astype(jnp.bfloat16)
        grad_in = jnp.dot(grad_pre, up_mat.T, preferred_element_type=jnp.float32).astype(jnp.bfloat16)
        grad_total = grad_total.at[flat_rows].add(grad_in.astype(jnp.float32), mode="drop")
        input_groups = inputs.reshape(DP_GROUPS, slot_rows, D).astype(jnp.float32)
        pre_groups = grad_pre.reshape(DP_GROUPS, slot_rows, H).astype(jnp.float32)
        outg_groups = grad_out.reshape(DP_GROUPS, slot_rows, D).astype(jnp.float32)
        act_groups = activated.reshape(DP_GROUPS, slot_rows, H).astype(jnp.float32)
        part_up = (jnp.einsum("nrd,nrh->ndh", input_groups, pre_groups) * grad_scale).astype(jnp.bfloat16)
        part_down = (jnp.einsum("nrd,nrh->ndh", outg_groups, act_groups) * grad_scale).astype(jnp.bfloat16)
        part_up = lax.optimization_barrier(part_up)
        part_down = lax.optimization_barrier(part_down)
        total_up = jnp.sum(part_up.astype(jnp.float32), axis=0)
        total_down = jnp.sum(part_down.astype(jnp.float32), axis=0)
        return (out_total, grad_total), (total_up, total_down)

    start = (jnp.zeros((TOKENS, D), jnp.float32), jnp.zeros((TOKENS, D), jnp.float32))
    (out_total, grad_total), (total_up, total_down) = lax.scan(
        one_expert, start, (token_table, coef_table, up_stack, down_stack))
    column = jnp.arange(EXPERTS, dtype=jnp.int32)
    holder = column // EXP_DEV
    slot_of = column % EXP_DEV
    anchor = jnp.where(slot_of == 0, partner[holder] * EXP_DEV, column).astype(jnp.int32)
    grad_up = jnp.moveaxis(total_up[anchor], 0, 1).astype(jnp.bfloat16)
    grad_down = jnp.moveaxis(total_down[anchor], 0, 1).astype(jnp.bfloat16)
    return (out_total.astype(jnp.bfloat16), grad_total.astype(jnp.bfloat16), grad_up, grad_down)
```

```python
import jax
import jax.numpy as jnp
from jax import lax
from jax.sharding import PartitionSpec as P

F32 = jnp.float32
BF16 = jnp.bfloat16


def swap(x, axis, mask):
    size = lax.axis_size(axis)
    return lax.ppermute(x, axis, [(i, i ^ mask) for i in range(size)])


def block_order(groups):
    top = groups // 2
    order = []
    bit = 1
    while bit < top:
        step = [m for m in range(groups) if m & bit and not m & (bit - 1)]
        order += [m for m in step if m & top] + [m for m in step if not m & top]
        bit *= 2
    return order + [top, 0]


def relative_cols(x, me, order):
    n = len(order)
    cols = x.shape[-1] // n
    blocks = [x[..., q * cols:(q + 1) * cols] for q in range(n)]
    bit = 1
    while bit < n:
        take = (me // bit) % 2 == 1
        blocks = [jnp.where(take, blocks[q ^ bit], blocks[q]) for q in range(n)]
        bit *= 2
    return [blocks[m] for m in order]


def absolute_cols(x, me, order):
    n = len(order)
    cols = x.shape[-1] // n
    blocks = [None] * n
    for place, m in enumerate(order):
        blocks[m] = x[..., place * cols:(place + 1) * cols]
    bit = 1
    while bit < n:
        take = (me // bit) % 2 == 1
        blocks = [jnp.where(take, blocks[q ^ bit], blocks[q]) for q in range(n)]
        bit *= 2
    return jnp.concatenate(blocks, axis=-1)


def gather_pair(first, second, bits):
    far = bits[:-1]
    parts = []
    for part, turn in ((first, 0), (second, 1)):
        axes = list(range(len(far)))
        axes = axes[turn:] + axes[:turn]
        part = part.reshape((1,) * len(far) + part.shape)
        for at in axes:
            part = jnp.concatenate([part, swap(part, "expert", far[at])], axis=at)
        parts.append(part)
    both = jnp.concatenate(parts, axis=-1)[None]
    both = jnp.concatenate([both, swap(both, "expert", bits[-1])], axis=0)
    return both.reshape((-1,) + both.shape[-2:])


def plus(a, b):
    return (a.astype(F32) + b.astype(F32)).astype(BF16)


def scatter_sum(x, bits):
    far = bits[:-1]
    x = x.reshape((2,) * len(bits) + x.shape[1:])
    x = plus(x[0], swap(x[1], "expert", bits[-1]))
    cols = x.shape[-1] // 2
    parts = []
    for part, turn in ((x[..., :cols], 0), (x[..., cols:], 1)):
        axes = list(range(len(far)))
        axes = axes[turn:] + axes[:turn]
        for at in axes:
            keep = lax.slice_in_dim(part, 0, 1, axis=at)
            send = lax.slice_in_dim(part, 1, 2, axis=at)
            part = plus(keep, swap(send, "expert", far[at]))
        parts.append(part.reshape(part.shape[-2:]))
    return jnp.concatenate(parts, axis=-1)


def dot(a, b, dims):
    return lax.dot_general(a, b, ((dims[0], dims[1]), ((), ())), preferred_element_type=F32)


def silu_slope(hidden_pre):
    sigma = jax.nn.sigmoid(hidden_pre)
    return sigma * (1.0 + hidden_pre * (1.0 - sigma))


def body(tokens, expert_ids, combine_weight, partner, w_up, w_down, out_grad):
    owners = lax.axis_size("expert")
    groups = lax.axis_size("dp")
    me_g = lax.axis_index("dp")
    me_j = lax.axis_index("expert")
    tok_dev, chosen = expert_ids.shape
    width = tokens.shape[1]
    slots = w_up.shape[1]
    hidden = w_up.shape[2]
    half = hidden // 2
    mine = slots * half
    experts = slots * owners
    rows = width // groups
    top = groups // 2
    upper = me_g // top == 1
    order = block_order(groups)
    bits = [owners >> (i + 1) for i in range(owners.bit_length() - 1)]

    named = expert_ids[:, :, None] == jnp.arange(experts, dtype=jnp.int32)[None, None, :]
    coef = jnp.sum(jnp.where(named, combine_weight[:, :, None], 0.0), axis=1)
    coef_hi = lax.reduce_precision(coef, 8, 7)
    coef_lo = coef - coef_hi
    lanes = -(-2 * experts // 128) * 128
    extra = jnp.pad(
        jnp.concatenate([coef_hi, coef_lo], axis=1), ((0, 0), (0, lanes - 2 * experts))
    ).astype(BF16)

    raw = jnp.concatenate([tokens, extra], axis=1)
    other_raw = swap(raw, "dp", top)
    other_grad = swap(lax.optimization_barrier((out_grad, other_raw))[0], "dp", top)

    def gather_tokens(x):
        parts = relative_cols(x[:, :width], me_g, order)
        at = groups // 2
        return gather_pair(
            jnp.concatenate(parts[:at], axis=1),
            jnp.concatenate(parts[at:] + [x[:, width:]], axis=1),
            bits,
        )

    x_own = gather_tokens(raw)
    other_raw, x_own = lax.optimization_barrier((other_raw, x_own))
    x_other = gather_tokens(other_raw)
    x_all = jnp.stack([x_own, x_other], axis=1).reshape(-1, width + lanes)
    x_own = x_own.reshape(-1, width + lanes)

    pair_grad = jnp.concatenate([out_grad, other_grad], axis=0)
    pair_grad, x_other = lax.optimization_barrier((pair_grad, x_other))
    grad_parts = relative_cols(pair_grad, me_g, order)
    at = groups // 2
    quarter = groups // 4 if groups >= 4 else 1

    def gather_grads(parts):
        mid = max(1, len(parts) // 2)
        first, second = parts[:mid], parts[mid:]
        if not second:
            cols = first[0].shape[1] // 2
            first, second = [first[0][:, :cols]], [first[0][:, cols:]]
        out = gather_pair(jnp.concatenate(first, axis=1), jnp.concatenate(second, axis=1), bits)
        return out.reshape(-1, out.shape[-1])

    g_send = gather_grads(grad_parts[:at])
    keep_parts, g_send = lax.optimization_barrier((grad_parts[at:], g_send))
    g_keep = gather_grads(keep_parts)
    g_halves = (g_send, g_keep)

    def arrange(w):
        w = jnp.concatenate(
            [lax.dynamic_slice_in_dim(w, (me_g ^ m) * rows, rows, axis=0) for m in order], axis=0
        )
        low = [w[:, s, :half] for s in range(slots)]
        high = [w[:, s, half:] for s in range(slots)]
        own = [jnp.where(upper, h, l) for l, h in zip(low, high)]
        rest = [jnp.where(upper, l, h) for l, h in zip(low, high)]
        return jnp.concatenate(own + rest, axis=1)

    up = arrange(w_up)
    down = arrange(w_down)

    def coefs(extra_cols):
        both = extra_cols[:, :experts].astype(F32) + extra_cols[:, experts:2 * experts].astype(F32)
        cols = []
        for s in range(slots):
            pick = jnp.arange(experts, dtype=jnp.int32)[None, :] == me_j * slots + s
            one = jnp.sum(jnp.where(pick, both, 0.0), axis=1, keepdims=True)
            cols.append(jnp.broadcast_to(one, (one.shape[0], half)))
        return jnp.concatenate(cols, axis=1)

    coef_all = coefs(x_all[:, width:])
    coef_own = coefs(x_own[:, width:])

    def own_rows(x):
        return x.reshape(owners, 2, tok_dev, x.shape[-1])[:, 0].reshape(owners * tok_dev, x.shape[-1])

    hid = dot(x_all[:, :width], up[:, :mine], ((1,), (0,)))
    act = (coef_all * jax.nn.silu(hid)).astype(BF16)

    def weight_grads(left, right):
        scale = 1.0 / tok_dev
        blocks = {}
        sends = {}
        for place, m in enumerate(order):
            part, at_col = divmod(place * rows, width // 2)
            cols = left[part][:, at_col:at_col + rows]
            blocks[m] = dot(cols, right, ((0,), (0,))) * scale
        bit = 1
        for m in order:
            if m == top or m == 0:
                continue
            bit = m & -m
            got = swap(blocks[m].astype(BF16), "dp", bit)
            blocks[m ^ bit] = blocks[m ^ bit] + got.astype(F32)
        got = swap(blocks[top].astype(BF16), "dp", top)
        own = blocks[0].astype(BF16)
        return [
            jnp.where(
                upper,
                jnp.concatenate([got[:, s * half:(s + 1) * half], own[:, s * half:(s + 1) * half]], axis=1),
                jnp.concatenate([own[:, s * half:(s + 1) * half], got[:, s * half:(s + 1) * half]], axis=1),
            )
            for s in range(slots)
        ]

    def relocated(per_slot):
        first = per_slot[0].reshape(owners, rows // owners, hidden)
        spread = lax.all_to_all(first, "expert", split_axis=0, concat_axis=0, tiled=True)
        moved = lax.all_to_all(spread[partner], "expert", split_axis=0, concat_axis=0, tiled=True)
        return jnp.stack([moved.reshape(rows, hidden)] + per_slot[1:], axis=1)

    grad_down = relocated(weight_grads(g_halves, act))

    split = width // 2
    back = dot(g_send, down[:split, :mine], ((1,), (0,))) + dot(g_keep, down[split:, :mine], ((1,), (0,)))
    pre = (coef_all * back * silu_slope(hid)).astype(BF16)
    grad_up = relocated(weight_grads((x_all[:, :split], x_all[:, split:width]), pre))

    hid_rest = dot(x_own[:, :width], up[:, mine:], ((1,), (0,)))
    act_rest = (coef_own * jax.nn.silu(hid_rest)).astype(BF16)
    act_full = jnp.concatenate([own_rows(act), act_rest], axis=1)
    part_out = dot(act_full, down, ((1,), (1,))).astype(BF16)
    output = absolute_cols(
        scatter_sum(part_out.reshape(owners, tok_dev, width), bits), me_g, order
    )
    back_rest = dot(own_rows(g_send), down[:split, mine:], ((1,), (0,))) + dot(
        own_rows(g_keep), down[split:, mine:], ((1,), (0,))
    )
    pre_rest = (coef_own * back_rest * silu_slope(hid_rest)).astype(BF16)
    pre_full = jnp.concatenate([own_rows(pre), pre_rest], axis=1)
    part_in = dot(pre_full, up, ((1,), (1,))).astype(BF16)
    input_grad = absolute_cols(
        scatter_sum(part_in.reshape(owners, tok_dev, width), bits), me_g, order
    )
    return (output, input_grad, grad_up, grad_down)


def solution(mesh):
    return jax.shard_map(
        body,
        mesh=mesh,
        in_specs=(
            P(("dp", "expert"), None),
            P(("dp", "expert"), None),
            P(("dp", "expert"), None),
            P(),
            P(None, "expert", None),
            P(None, "expert", None),
            P(("dp", "expert"), None),
        ),
        out_specs=(
            P(("dp", "expert"), None),
            P(("dp", "expert"), None),
            P("dp", "expert", None),
            P("dp", "expert", None),
        ),
        check_vma=False,
    )
```

```python
import functools

import jax
import jax.numpy as jnp
from jax import lax
from jax.experimental import pallas as pl
from jax.experimental.pallas import tpu as pltpu
from jax.sharding import PartitionSpec as P

F32 = jnp.float32
BF16 = jnp.bfloat16
MIB = 1 << 20


def swap(x, axis, mask):
    size = lax.axis_size(axis)
    return lax.ppermute(x, axis, [(i, i ^ mask) for i in range(size)])


def zero_of(x):
    first = lax.slice(x, (0,) * x.ndim, (1,) * x.ndim).reshape(()).astype(F32)
    return jnp.minimum(jnp.abs(first), 0.0)


def after(x, *given):
    total = sum(zero_of(one) for one in given)
    return x + total.astype(x.dtype)


def block_order(groups):
    top = groups // 2
    order = []
    bit = 1
    while bit < top:
        step = [m for m in range(groups) if m & bit and not m & (bit - 1)]
        order += [m for m in step if m & top] + [m for m in step if not m & top]
        bit *= 2
    return order + [top, 0]


def relative_cols(x, me, order):
    n = len(order)
    cols = x.shape[-1] // n
    blocks = [x[..., q * cols:(q + 1) * cols] for q in range(n)]
    bit = 1
    while bit < n:
        take = (me // bit) % 2 == 1
        blocks = [jnp.where(take, blocks[q ^ bit], blocks[q]) for q in range(n)]
        bit *= 2
    return [blocks[m] for m in order]


def gather_parts(parts, bits):
    far = bits[:-1]
    out = []
    early = None
    for turn, part in enumerate(parts):
        axes = list(range(len(far)))
        axes = axes[turn % 2:] + axes[:turn % 2]
        planes = part.shape[0]
        part = part.reshape((planes,) + (1,) * len(bits) + part.shape[1:])
        for at in axes:
            got = swap(part, "expert", far[at])
            early = got if early is None else early
            part = jnp.concatenate([part, got], axis=at + 2)
        part = jnp.concatenate([part, swap(part, "expert", bits[-1])], axis=1)
        out.append(part.reshape(-1, part.shape[-1]))
    return out, early


def plus(a, b):
    return (a.astype(F32) + b.astype(F32)).astype(BF16)


def scatter_sum(x, bits):
    far = bits[:-1]
    x = x.reshape((2,) * len(bits) + x.shape[1:])
    x = plus(x[0], swap(x[1], "expert", bits[-1]))
    cols = x.shape[-1] // 2
    parts = []
    for part, turn in ((x[..., :cols], 0), (x[..., cols:], 1)):
        axes = list(range(len(far)))
        axes = axes[turn:] + axes[:turn]
        for at in axes:
            keep = lax.slice_in_dim(part, 0, 1, axis=at)
            send = lax.slice_in_dim(part, 1, 2, axis=at)
            part = plus(keep, swap(send, "expert", far[at]))
        parts.append(part.reshape(part.shape[-2:]))
    return jnp.concatenate(parts, axis=-1)


def load_weights(place, weight, buffer, sems, blocks, half_index):
    slots, width, hidden = weight.shape
    rows, half = width // blocks, hidden // 2
    copies = []
    for i in range(blocks):
        for s in range(slots):
            copies.append(
                pltpu.make_async_copy(
                    weight.at[
                        s,
                        pl.ds(pl.multiple_of(place[i] * rows, rows), rows),
                        pl.ds(pl.multiple_of(half_index * half, half), half),
                    ],
                    buffer.at[pl.ds(i * rows, rows), pl.ds(s * half, half)],
                    sems.at[i * slots + s],
                )
            )
    for copy in copies:
        copy.start()
    for copy in copies:
        copy.wait()


def hidden_kernel(blocks, experts, place, first, second, weight, *rest):
    act, slope, buffer, sems = rest[-4:]
    slots = weight.shape[0]
    split = first.shape[1]
    width = weight.shape[1]

    @pl.when(pl.program_id(0) == 0)
    def _():
        load_weights(place, weight, buffer, sems, blocks, place[blocks])

    pre = jnp.dot(first[...], buffer[:split], preferred_element_type=F32) + jnp.dot(
        second[:, :width - split], buffer[split:], preferred_element_type=F32
    )
    coefs = second[:, width - split:].astype(F32)
    lane = lax.broadcasted_iota(jnp.int32, coefs.shape, 1)
    half = pre.shape[1] // slots
    for s in range(slots):
        wanted = place[blocks + 1] * slots + s
        named = (lane == wanted) | (lane == wanted + experts)
        coef = jnp.sum(jnp.where(named, coefs, 0.0), axis=1, keepdims=True)
        one = pre[:, s * half:(s + 1) * half]
        sigma = 1.0 / (1.0 + jnp.exp(-one))
        act[:, s * half:(s + 1) * half] = (coef * (one * sigma)).astype(BF16)
        slope[:, s * half:(s + 1) * half] = (coef * (sigma * (1.0 + one * (1.0 - sigma)))).astype(BF16)


def hidden_product(place, parts, weight, experts, total_rows, at_row, filled=None, tile=256):
    first, second = parts
    slots, width, hidden = weight.shape
    blocks = place.shape[0] - 2
    cols = slots * hidden // 2
    rows = first.shape[0]
    skip = at_row // tile
    shape = jax.ShapeDtypeStruct((total_rows, cols), BF16)
    any_space = pl.BlockSpec(memory_space=pl.ANY)
    given = () if filled is None else tuple(filled)
    return pl.pallas_call(
        functools.partial(hidden_kernel, blocks, experts),
        out_shape=[shape, shape],
        grid_spec=pltpu.PrefetchScalarGridSpec(
            num_scalar_prefetch=1,
            grid=(rows // tile,),
            in_specs=[
                pl.BlockSpec((tile, first.shape[1]), lambda i, p: (i, 0)),
                pl.BlockSpec((tile, second.shape[1]), lambda i, p: (i, 0)),
                any_space,
            ]
            + [any_space] * len(given),
            out_specs=[pl.BlockSpec((tile, cols), lambda i, p: (i + skip, 0))] * 2,
            scratch_shapes=[
                pltpu.VMEM((width, cols), BF16),
                pltpu.SemaphoreType.DMA((blocks * slots,)),
            ],
        ),
        input_output_aliases={4: 0, 5: 1} if given else {},
        compiler_params=pltpu.CompilerParams(vmem_limit_bytes=24 * MIB),
        cost_estimate=pl.CostEstimate(
            flops=2 * rows * width * cols,
            bytes_accessed=2 * (rows * width + width * cols + 2 * rows * cols),
            transcendentals=rows * cols,
        ),
        name="hidden_product",
    )(place, first, second, weight, *given)


def back_kernel(blocks, count, place, *refs):
    parts, (weight, slope, out, buffer, sems) = refs[:count], refs[count:]

    @pl.when(pl.program_id(0) == 0)
    def _():
        load_weights(place, weight, buffer, sems, blocks, place[blocks])

    total = None
    at = 0
    for part in parts:
        depth = part.shape[1]
        term = jnp.dot(part[...], buffer[at:at + depth], preferred_element_type=F32)
        total = term if total is None else total + term
        at += depth
    out[...] = (total * slope[...].astype(F32)).astype(BF16)


def back_product(place, parts, weight, slope, tile=256):
    slots, width, hidden = weight.shape
    blocks = place.shape[0] - 2
    cols = slots * hidden // 2
    rows = slope.shape[0]
    return pl.pallas_call(
        functools.partial(back_kernel, blocks, len(parts)),
        out_shape=jax.ShapeDtypeStruct((rows, cols), BF16),
        grid_spec=pltpu.PrefetchScalarGridSpec(
            num_scalar_prefetch=1,
            grid=(rows // tile,),
            in_specs=[pl.BlockSpec((tile, part.shape[1]), lambda i, p: (i, 0)) for part in parts]
            + [pl.BlockSpec(memory_space=pl.ANY), pl.BlockSpec((tile, cols), lambda i, p: (i, 0))],
            out_specs=pl.BlockSpec((tile, cols), lambda i, p: (i, 0)),
            scratch_shapes=[
                pltpu.VMEM((width, cols), BF16),
                pltpu.SemaphoreType.DMA((blocks * slots,)),
            ],
        ),
        compiler_params=pltpu.CompilerParams(vmem_limit_bytes=24 * MIB),
        cost_estimate=pl.CostEstimate(
            flops=2 * rows * width * cols,
            bytes_accessed=2 * (rows * width + width * cols + 2 * rows * cols),
            transcendentals=0,
        ),
        name="back_product",
    )(place, *parts, weight, slope)


def out_kernel(place, own, rest, weight, out, buffer, sems):
    slots, _, hidden = weight.shape
    half = hidden // 2
    rows = out.shape[0]

    @pl.when(pl.program_id(0) == 0)
    def _():
        copies = []
        for s in range(slots):
            for k, (source, index) in enumerate(((own, place[0]), (rest, 1 - place[0]))):
                copies.append(
                    pltpu.make_async_copy(
                        source.at[pl.ds(0, rows), pl.ds(s * half, half)],
                        buffer.at[s, :, pl.ds(pl.multiple_of(index * half, half), half)],
                        sems.at[2 * s + k],
                    )
                )
        for copy in copies:
            copy.start()
        for copy in copies:
            copy.wait()

    total = None
    for s in range(slots):
        term = lax.dot_general(
            buffer[s], weight[s], (((1,), (1,)), ((), ())), preferred_element_type=F32
        )
        total = term if total is None else total + term
    out[...] = total.astype(BF16)


def out_product(half_index, own, rest, weight, tile=256):
    slots, width, hidden = weight.shape
    rows = rest.shape[0]
    return pl.pallas_call(
        out_kernel,
        out_shape=jax.ShapeDtypeStruct((rows, width), BF16),
        grid_spec=pltpu.PrefetchScalarGridSpec(
            num_scalar_prefetch=1,
            grid=(width // tile,),
            in_specs=[
                pl.BlockSpec(memory_space=pl.ANY),
                pl.BlockSpec(memory_space=pl.ANY),
                pl.BlockSpec((slots, tile, hidden), lambda i, p: (0, i, 0)),
            ],
            out_specs=pl.BlockSpec((rows, tile), lambda i, p: (0, i)),
            scratch_shapes=[
                pltpu.VMEM((slots, rows, hidden), BF16),
                pltpu.SemaphoreType.DMA((2 * slots,)),
            ],
        ),
        compiler_params=pltpu.CompilerParams(vmem_limit_bytes=24 * MIB),
        cost_estimate=pl.CostEstimate(
            flops=2 * rows * width * slots * hidden,
            bytes_accessed=2 * (rows * width + width * slots * hidden + rows * slots * hidden),
            transcendentals=0,
        ),
        name="out_product",
    )(half_index, own, rest, weight)


def outer(left, right):
    return lax.dot_general(left, right, (((0,), (0,)), ((), ())), preferred_element_type=F32)


def body(tokens, expert_ids, combine_weight, partner, w_up, w_down, out_grad):
    owners = lax.axis_size("expert")
    groups = lax.axis_size("dp")
    me_g = lax.axis_index("dp")
    me_j = lax.axis_index("expert")
    tok_dev, chosen = expert_ids.shape
    width = tokens.shape[1]
    slots = w_up.shape[1]
    hidden = w_up.shape[2]
    half = hidden // 2
    experts = slots * owners
    rows = width // groups
    top = groups // 2
    upper = me_g // top == 1
    upper_index = (me_g // top).astype(jnp.int32)
    order = block_order(groups)
    bits = [owners >> (i + 1) for i in range(owners.bit_length() - 1)]
    plane = owners * tok_dev
    scale = 1.0 / tok_dev

    named = expert_ids[:, :, None] == jnp.arange(experts, dtype=jnp.int32)[None, None, :]
    coef = jnp.sum(jnp.where(named, combine_weight[:, :, None], 0.0), axis=1)
    coef_hi = lax.reduce_precision(coef, 8, 7)
    coef_lo = coef - coef_hi
    lanes = -(-2 * experts // 128) * 128
    extra = jnp.pad(
        jnp.concatenate([coef_hi, coef_lo], axis=1), ((0, 0), (0, lanes - 2 * experts))
    ).astype(BF16)

    raw = jnp.concatenate([tokens, extra], axis=1)
    other_raw = swap(raw, "dp", top)
    other_grad = swap(after(out_grad, other_raw), "dp", top)

    def token_parts(x):
        blocks = relative_cols(x[:, :width], me_g, order)
        first = jnp.concatenate(blocks[:groups // 2], axis=1)
        second = jnp.concatenate(blocks[groups // 2:] + [x[:, width:]], axis=1)
        return [first[None], second[None]]

    x_own, _ = gather_parts(token_parts(raw), bits)
    x_other, early = gather_parts(token_parts(other_raw), bits)

    pair_grad = jnp.stack([out_grad, other_grad], axis=0)
    blocks = relative_cols(after(pair_grad, early), me_g, order)
    per = groups // 4
    quarters = [jnp.concatenate(blocks[i * per:(i + 1) * per], axis=-1) for i in range(4)]
    g_send, early = gather_parts(quarters[:2], bits)
    g_keep, _ = gather_parts([after(one, early) for one in quarters[2:]], bits)
    g_parts = g_send + g_keep

    up = jnp.swapaxes(w_up, 0, 1)
    down = jnp.swapaxes(w_down, 0, 1)

    offsets = jnp.stack([me_g ^ m for m in order]).astype(jnp.int32)
    me_word = me_j.astype(jnp.int32)

    def place_of(half_index):
        return jnp.concatenate([offsets, half_index[None], me_word[None]])

    place = place_of(upper_index)
    both = hidden_product(place, x_own, up, experts, 2 * plane, 0)
    act, slope = hidden_product(place, x_other, up, experts, 2 * plane, plane, both)

    def down_block(m):
        part, col = divmod(order.index(m) * rows, width // 4)
        return outer(g_parts[part][:, col:col + rows], act) * scale

    def reduced(block_of, split, ahead=None):
        pieces = slots if split else 1
        wide = slots * half // pieces
        cut = lambda x: [x[:, i * wide:(i + 1) * wide] for i in range(pieces)]
        sends = {m: cut(block_of(m).astype(BF16)) for m in order if m & (top - 1)}
        if ahead is not None:
            ahead.append(sends[order[len(sends) - 1]][0])
        kept = {m: block_of(m) for m in (top, 0)}
        kept = {m: cut(x) for m, x in kept.items()}
        own, got = [], []
        for i in range(pieces):
            have = {m: sends[m][i] for m in sends}
            for m in sends:
                bit = m & -m
                piece = swap(have[m], "dp", bit)
                to = m ^ bit
                if to in kept:
                    kept[to][i] = kept[to][i] + piece.astype(F32)
                else:
                    have[to] = plus(have[to], piece)
            own.append(kept[0][i].astype(BF16))
            got.append(swap(kept[top][i].astype(BF16), "dp", top))
        own = own if split else [own[0][:, s * half:(s + 1) * half] for s in range(slots)]
        got = got if split else [got[0][:, s * half:(s + 1) * half] for s in range(slots)]
        return [
            jnp.where(upper, jnp.concatenate([b, a], axis=1), jnp.concatenate([a, b], axis=1))
            for a, b in zip(own, got)
        ]

    def relocated(per_slot):
        first = per_slot[0].reshape(owners, rows // owners, hidden)
        spread = lax.all_to_all(first, "expert", split_axis=0, concat_axis=0, tiled=True)
        moved = lax.all_to_all(spread[partner], "expert", split_axis=0, concat_axis=0, tiled=True)
        return jnp.stack([moved.reshape(rows, hidden)] + per_slot[1:], axis=1)

    down_sent = []
    grad_down = relocated(reduced(down_block, False, down_sent))

    place = place + zero_of(down_sent[0]).astype(jnp.int32)
    pre = back_product(place, g_parts, down, slope)

    def up_block(m):
        part, col = divmod(order.index(m) * rows, width // 2)
        return (
            outer(x_own[part][:, col:col + rows], pre[:plane])
            + outer(x_other[part][:, col:col + rows], pre[plane:])
        ) * scale

    up_sent = []
    grad_up = relocated(reduced(up_block, True, up_sent))

    later = zero_of(up_sent[0]).astype(jnp.int32)
    rest_place = place_of(1 - upper_index) + later
    half_index = upper_index[None] + later
    act_rest, slope_rest = hidden_product(rest_place, x_own, up, experts, plane, 0)
    part_out = out_product(half_index, act, act_rest, down)
    output = scatter_sum(part_out.reshape(owners, tok_dev, width), bits)
    pre_rest = back_product(rest_place, g_parts, down, slope_rest)
    part_in = out_product(half_index, pre, pre_rest, up)
    input_grad = scatter_sum(part_in.reshape(owners, tok_dev, width), bits)
    return (output, input_grad, grad_up, grad_down)


def solution(mesh):
    return jax.shard_map(
        body,
        mesh=mesh,
        in_specs=(
            P(("dp", "expert"), None),
            P(("dp", "expert"), None),
            P(("dp", "expert"), None),
            P(),
            P(None, "expert", None),
            P(None, "expert", None),
            P(("dp", "expert"), None),
        ),
        out_specs=(
            P(("dp", "expert"), None),
            P(("dp", "expert"), None),
            P("dp", "expert", None),
            P("dp", "expert", None),
        ),
        check_vma=False,
    )
```

```python
import functools

import jax
import jax.numpy as jnp
from jax import lax
from jax.experimental import pallas as pl
from jax.experimental.pallas import tpu as pltpu
from jax.sharding import PartitionSpec as P

F32 = jnp.float32
BF16 = jnp.bfloat16
MIB = 1 << 20


def swap(x, axis, mask):
    size = lax.axis_size(axis)
    return lax.ppermute(x, axis, [(i, i ^ mask) for i in range(size)])


def nothing_kernel(*refs):
    del refs


def after(x, *given):
    any_space = pl.BlockSpec(memory_space=pl.ANY)
    return pl.pallas_call(
        nothing_kernel,
        out_shape=jax.ShapeDtypeStruct(x.shape, x.dtype),
        in_specs=[any_space] * (1 + len(given)),
        out_specs=any_space,
        input_output_aliases={0: 0},
        cost_estimate=pl.CostEstimate(flops=0, bytes_accessed=0, transcendentals=0),
        name="after",
    )(x, *given)


def block_order(groups):
    top = groups // 2
    odd = [m for m in range(top) if m & 1]
    even = [m for m in range(top - 1, -1, -1) if not m & 1]
    return [m | top for m in odd] + odd + [m | top for m in even] + even


def relative_cols(x, me, order):
    n = len(order)
    cols = x.shape[-1] // n
    blocks = [x[..., q * cols:(q + 1) * cols] for q in range(n)]
    bit = 1
    while bit < n:
        take = (me // bit) % 2 == 1
        blocks = [jnp.where(take, blocks[q ^ bit], blocks[q]) for q in range(n)]
        bit *= 2
    return [blocks[m] for m in order]


def gather_parts(parts, bits):
    far = bits[:-1]
    out = []
    early = None
    for turn, part in enumerate(parts):
        axes = list(range(len(far)))
        axes = axes[turn % 2:] + axes[:turn % 2]
        planes = part.shape[0]
        part = part.reshape((planes,) + (1,) * len(bits) + part.shape[1:])
        for at in axes:
            got = swap(part, "expert", far[at])
            early = got if early is None else early
            part = jnp.concatenate([part, got], axis=at + 2)
        part = jnp.concatenate([part, swap(part, "expert", bits[-1])], axis=1)
        out.append(part.reshape(-1, part.shape[-1]))
    return out, early


def plus(a, b):
    return (a.astype(F32) + b.astype(F32)).astype(BF16)


def core_sum(x, bits):
    x = x.reshape((2, x.shape[0] // 2) + x.shape[1:])
    return plus(x[0], swap(x[1], "expert", bits[-1]))


def far_sum(x, bits):
    total = x[0].astype(F32)
    for m in range(1, x.shape[0]):
        total = total + swap(x[m], "expert", m * 2).astype(F32)
    return total.astype(BF16)


def load_weights(place, weight, buffer, sems, blocks, half_index):
    slots, width, hidden = weight.shape
    rows, half = width // blocks, hidden // 2
    copies = []
    for i in range(blocks):
        for s in range(slots):
            copies.append(
                pltpu.make_async_copy(
                    weight.at[
                        s,
                        pl.ds(pl.multiple_of(place[i] * rows, rows), rows),
                        pl.ds(pl.multiple_of(half_index * half, half), half),
                    ],
                    buffer.at[pl.ds(i * rows, rows), pl.ds(s * half, half)],
                    sems.at[i * slots + s],
                )
            )
    for copy in copies:
        copy.start()
    for copy in copies:
        copy.wait()


def hidden_kernel(blocks, experts, place, first, second, weight, *rest):
    act, slope, buffer, sems = rest[-4:]
    slots = weight.shape[0]
    split = first.shape[1]
    width = weight.shape[1]

    @pl.when(pl.program_id(0) == 0)
    def _():
        load_weights(place, weight, buffer, sems, blocks, place[blocks])

    pre = jnp.dot(first[...], buffer[:split], preferred_element_type=F32) + jnp.dot(
        second[:, :width - split], buffer[split:], preferred_element_type=F32
    )
    coefs = second[:, width - split:].astype(F32)
    lane = lax.broadcasted_iota(jnp.int32, coefs.shape, 1)
    half = pre.shape[1] // slots
    for s in range(slots):
        wanted = place[blocks + 1] * slots + s
        named = (lane == wanted) | (lane == wanted + experts)
        coef = jnp.sum(jnp.where(named, coefs, 0.0), axis=1, keepdims=True)
        one = pre[:, s * half:(s + 1) * half]
        sigma = 1.0 / (1.0 + jnp.exp(-one))
        act[:, s * half:(s + 1) * half] = (coef * (one * sigma)).astype(BF16)
        slope[:, s * half:(s + 1) * half] = (coef * (sigma * (1.0 + one * (1.0 - sigma)))).astype(BF16)


def hidden_product(place, parts, weight, experts, total_rows, at_row, filled=None, given=(), tile=256):
    first, second = parts
    slots, width, hidden = weight.shape
    blocks = place.shape[0] - 2
    cols = slots * hidden // 2
    rows = first.shape[0]
    skip = at_row // tile
    shape = jax.ShapeDtypeStruct((total_rows, cols), BF16)
    any_space = pl.BlockSpec(memory_space=pl.ANY)
    held = () if filled is None else tuple(filled)
    return pl.pallas_call(
        functools.partial(hidden_kernel, blocks, experts),
        out_shape=[shape, shape],
        grid_spec=pltpu.PrefetchScalarGridSpec(
            num_scalar_prefetch=1,
            grid=(rows // tile,),
            in_specs=[
                pl.BlockSpec((tile, first.shape[1]), lambda i, p: (i, 0)),
                pl.BlockSpec((tile, second.shape[1]), lambda i, p: (i, 0)),
                any_space,
            ]
            + [any_space] * (len(held) + len(given)),
            out_specs=[pl.BlockSpec((tile, cols), lambda i, p: (i + skip, 0))] * 2,
            scratch_shapes=[
                pltpu.VMEM((width, cols), BF16),
                pltpu.SemaphoreType.DMA((blocks * slots,)),
            ],
        ),
        input_output_aliases={4: 0, 5: 1} if held else {},
        compiler_params=pltpu.CompilerParams(vmem_limit_bytes=24 * MIB),
        cost_estimate=pl.CostEstimate(
            flops=2 * rows * width * cols,
            bytes_accessed=2 * (rows * width + width * cols + 2 * rows * cols),
            transcendentals=rows * cols,
        ),
        name="hidden_product",
    )(place, first, second, weight, *held, *given)


def back_kernel(blocks, count, place, *refs):
    parts, weight, slope = refs[:count], refs[count], refs[count + 1]
    out, buffer, sems = refs[-3:]

    @pl.when(pl.program_id(0) == 0)
    def _():
        load_weights(place, weight, buffer, sems, blocks, place[blocks])

    total = None
    at = 0
    for part in parts:
        depth = part.shape[1]
        term = jnp.dot(part[...], buffer[at:at + depth], preferred_element_type=F32)
        total = term if total is None else total + term
        at += depth
    out[...] = (total * slope[...].astype(F32)).astype(BF16)


def back_product(place, parts, weight, slope, given=(), tile=256):
    slots, width, hidden = weight.shape
    blocks = place.shape[0] - 2
    cols = slots * hidden // 2
    rows = slope.shape[0]
    return pl.pallas_call(
        functools.partial(back_kernel, blocks, len(parts)),
        out_shape=jax.ShapeDtypeStruct((rows, cols), BF16),
        grid_spec=pltpu.PrefetchScalarGridSpec(
            num_scalar_prefetch=1,
            grid=(rows // tile,),
            in_specs=[pl.BlockSpec((tile, part.shape[1]), lambda i, p: (i, 0)) for part in parts]
            + [pl.BlockSpec(memory_space=pl.ANY), pl.BlockSpec((tile, cols), lambda i, p: (i, 0))]
            + [pl.BlockSpec(memory_space=pl.ANY)] * len(given),
            out_specs=pl.BlockSpec((tile, cols), lambda i, p: (i, 0)),
            scratch_shapes=[
                pltpu.VMEM((width, cols), BF16),
                pltpu.SemaphoreType.DMA((blocks * slots,)),
            ],
        ),
        compiler_params=pltpu.CompilerParams(vmem_limit_bytes=24 * MIB),
        cost_estimate=pl.CostEstimate(
            flops=2 * rows * width * cols,
            bytes_accessed=2 * (rows * width + width * cols + 2 * rows * cols),
            transcendentals=0,
        ),
        name="back_product",
    )(place, *parts, weight, slope, *given)


def out_kernel(place, own, rest, weight, out, buffer, sems):
    slots, _, hidden = weight.shape
    half = hidden // 2
    rows = out.shape[0]

    @pl.when(pl.program_id(0) == 0)
    def _():
        copies = []
        for s in range(slots):
            for k, (source, index) in enumerate(((own, place[0]), (rest, 1 - place[0]))):
                copies.append(
                    pltpu.make_async_copy(
                        source.at[pl.ds(0, rows), pl.ds(s * half, half)],
                        buffer.at[s, :, pl.ds(pl.multiple_of(index * half, half), half)],
                        sems.at[2 * s + k],
                    )
                )
        for copy in copies:
            copy.start()
        for copy in copies:
            copy.wait()

    total = None
    for s in range(slots):
        term = lax.dot_general(
            buffer[s], weight[s], (((1,), (1,)), ((), ())), preferred_element_type=F32
        )
        total = term if total is None else total + term
    out[...] = total.astype(BF16)


def out_product(half_index, own, rest, weight, tile=256):
    slots, width, hidden = weight.shape
    rows = rest.shape[0]
    return pl.pallas_call(
        out_kernel,
        out_shape=jax.ShapeDtypeStruct((rows, width), BF16),
        grid_spec=pltpu.PrefetchScalarGridSpec(
            num_scalar_prefetch=1,
            grid=(width // tile,),
            in_specs=[
                pl.BlockSpec(memory_space=pl.ANY),
                pl.BlockSpec(memory_space=pl.ANY),
                pl.BlockSpec((slots, tile, hidden), lambda i, p: (0, i, 0)),
            ],
            out_specs=pl.BlockSpec((rows, tile), lambda i, p: (0, i)),
            scratch_shapes=[
                pltpu.VMEM((slots, rows, hidden), BF16),
                pltpu.SemaphoreType.DMA((2 * slots,)),
            ],
        ),
        compiler_params=pltpu.CompilerParams(vmem_limit_bytes=24 * MIB),
        cost_estimate=pl.CostEstimate(
            flops=2 * rows * width * slots * hidden,
            bytes_accessed=2 * (rows * width + width * slots * hidden + rows * slots * hidden),
            transcendentals=0,
        ),
        name="out_product",
    )(half_index, own, rest, weight)


def outer(left, right):
    return lax.dot_general(left, right, (((0,), (0,)), ((), ())), preferred_element_type=F32)


def body(tokens, expert_ids, combine_weight, partner, w_up, w_down, out_grad):
    owners = lax.axis_size("expert")
    groups = lax.axis_size("dp")
    me_g = lax.axis_index("dp")
    me_j = lax.axis_index("expert")
    tok_dev, chosen = expert_ids.shape
    width = tokens.shape[1]
    slots = w_up.shape[1]
    hidden = w_up.shape[2]
    half = hidden // 2
    experts = slots * owners
    rows = width // groups
    top = groups // 2
    upper = me_g // top == 1
    upper_index = (me_g // top).astype(jnp.int32)
    order = block_order(groups)
    bits = [owners >> (i + 1) for i in range(owners.bit_length() - 1)]
    plane = owners * tok_dev
    scale = 1.0 / tok_dev

    named = expert_ids[:, :, None] == jnp.arange(experts, dtype=jnp.int32)[None, None, :]
    coef = jnp.sum(jnp.where(named, combine_weight[:, :, None], 0.0), axis=1)
    coef_hi = lax.reduce_precision(coef, 8, 7)
    coef_lo = coef - coef_hi
    lanes = -(-2 * experts // 128) * 128
    extra = jnp.pad(
        jnp.concatenate([coef_hi, coef_lo], axis=1), ((0, 0), (0, lanes - 2 * experts))
    ).astype(BF16)

    quarter = groups // 4

    def quarters(x):
        blocks = relative_cols(x, me_g, order)
        return [jnp.concatenate(blocks[i * quarter:(i + 1) * quarter], axis=-1) for i in range(4)]

    token_quarters = quarters(tokens)
    own_first = jnp.concatenate(token_quarters[:2], axis=1)[None]
    own_second = jnp.concatenate(token_quarters[2:] + [extra], axis=1)[None]
    x_own, early = gather_parts([own_first, own_second], bits)
    other_first = swap(own_first, "dp", top)
    other_second = swap(own_second, "dp", top)
    x_other, early = gather_parts([other_first, other_second], bits)

    own_grads = quarters(out_grad)
    got_send = swap(after(jnp.concatenate(own_grads[:2], axis=1), other_first), "dp", top)
    got_keep = swap(after(jnp.concatenate(own_grads[2:], axis=1), other_second), "dp", top)

    def pair(own, got):
        cols = own[0].shape[1]
        return [jnp.stack([own[i], got[:, (1 - i) * cols:(2 - i) * cols]], axis=0) for i in range(2)]

    g_send, early = gather_parts([after(one, early) for one in pair(own_grads[:2], got_send)], bits)
    g_keep, _ = gather_parts([after(one, early) for one in pair(own_grads[2:], got_keep)], bits)
    g_parts = g_send + g_keep

    up = jnp.swapaxes(w_up, 0, 1)
    down = jnp.swapaxes(w_down, 0, 1)

    offsets = jnp.stack([me_g ^ m for m in order]).astype(jnp.int32)
    me_word = me_j.astype(jnp.int32)

    def place_of(half_index, change=0):
        return jnp.concatenate([offsets ^ change, half_index[None], me_word[None]])

    place = place_of(upper_index)
    both = hidden_product(place, x_own, up, experts, 2 * plane, 0)
    act, slope = hidden_product(place_of(upper_index, top), x_other, up, experts, 2 * plane, plane, both)

    def down_block(m):
        part, col = divmod(order.index(m) * rows, width // 4)
        return outer(g_parts[part][:, col:col + rows], act) * scale

    def cut(x, pieces):
        wide = x.shape[1] // pieces
        return [x[:, i * wide:(i + 1) * wide] for i in range(pieces)]

    def sent_blocks(block_of, pieces):
        return {m: cut(block_of(m).astype(BF16), pieces) for m in order if m & (top - 1)}

    def reduced(sends, block_of, pieces, ready):
        kept = {m: cut(block_of(m), pieces) for m in (top, 0)}
        for i in range(pieces):
            have = {m: sends[m][i] for m in sends}
            for m in sends:
                bit = m & -m
                piece = swap(have[m], "dp", bit)
                to = m ^ bit
                if to in kept:
                    kept[to][i] = kept[to][i] + piece.astype(F32)
                else:
                    have[to] = plus(have[to], piece)
        leaving = [x.astype(BF16) for x in kept[top]]
        own = [x.astype(BF16) for x in kept[0]]
        return own, [ready(x) for x in leaving]

    def whole(own, leaving, pieces):
        got = [swap(x, "dp", top) for x in leaving]
        if pieces == 1:
            own, got = cut(own[0], slots), cut(got[0], slots)
        return [
            jnp.where(upper, jnp.concatenate([b, a], axis=1), jnp.concatenate([a, b], axis=1))
            for a, b in zip(own, got)
        ]

    def relocated(per_slot):
        first = per_slot[0].reshape(owners, rows // owners, hidden)
        spread = lax.all_to_all(first, "expert", split_axis=0, concat_axis=0, tiled=True)
        moved = lax.all_to_all(spread[partner], "expert", split_axis=0, concat_axis=0, tiled=True)
        return jnp.stack([moved.reshape(rows, hidden)] + per_slot[1:], axis=1)

    down_sends = sent_blocks(down_block, 1)
    pre = back_product(place, g_parts, down, slope, given=[x[0] for x in down_sends.values()])

    def up_block(m):
        part, col = divmod(order.index(m) * rows, width // 2)
        other_part, other_col = divmod(order.index(m ^ top) * rows, width // 2)
        return (
            outer(x_own[part][:, col:col + rows], pre[:plane])
            + outer(x_other[other_part][:, other_col:other_col + rows], pre[plane:])
        ) * scale

    up_sends = sent_blocks(up_block, slots)
    down_own, down_leaving = reduced(down_sends, down_block, 1, lambda x: x)

    rest_place = place_of(1 - upper_index)
    act_rest, slope_rest = hidden_product(
        rest_place, x_own, up, experts, plane, 0, given=down_leaving + [x[-1] for x in up_sends.values()]
    )
    part_out = out_product(upper_index[None], act, act_rest, down)
    out_core = core_sum(part_out.reshape(owners, tok_dev, width), bits)
    pre_rest = back_product(rest_place, g_parts, down, slope_rest)
    part_in = out_product(upper_index[None], pre, pre_rest, up)
    in_core = core_sum(part_in.reshape(owners, tok_dev, width), bits)

    up_own, up_leaving = reduced(up_sends, up_block, slots, lambda x: after(x, out_core))
    up_leaving = up_leaving[:-1] + [after(up_leaving[-1], in_core)]
    grad_down = relocated(whole(down_own, down_leaving, 1))
    grad_up = relocated(whole(up_own, up_leaving, slots))
    output = far_sum(out_core, bits)
    input_grad = far_sum(in_core, bits)
    return (output, input_grad, grad_up, grad_down)


def solution(mesh):
    return jax.shard_map(
        body,
        mesh=mesh,
        in_specs=(
            P(("dp", "expert"), None),
            P(("dp", "expert"), None),
            P(("dp", "expert"), None),
            P(),
            P(None, "expert", None),
            P(None, "expert", None),
            P(("dp", "expert"), None),
        ),
        out_specs=(
            P(("dp", "expert"), None),
            P(("dp", "expert"), None),
            P("dp", "expert", None),
            P("dp", "expert", None),
        ),
        check_vma=False,
    )
```

```python
import functools

import jax
import jax.numpy as jnp
from jax import lax
from jax.experimental import pallas as pl
from jax.experimental.pallas import tpu as pltpu
from jax.sharding import PartitionSpec as P

F32 = jnp.float32
BF16 = jnp.bfloat16
MIB = 1 << 20


def swap(x, axis, mask):
    size = lax.axis_size(axis)
    return lax.ppermute(x, axis, [(i, i ^ mask) for i in range(size)])


def nothing_kernel(*refs):
    del refs


def after(x, *given):
    any_space = pl.BlockSpec(memory_space=pl.ANY)
    return pl.pallas_call(
        nothing_kernel,
        out_shape=jax.ShapeDtypeStruct(x.shape, x.dtype),
        in_specs=[any_space] * (1 + len(given)),
        out_specs=any_space,
        input_output_aliases={0: 0},
        cost_estimate=pl.CostEstimate(flops=0, bytes_accessed=0, transcendentals=0),
        name="after",
    )(x, *given)


def block_order(groups):
    top = groups // 2
    odd = [m for m in range(top) if m & 1]
    even = [m for m in range(top - 1, -1, -1) if not m & 1]
    return [m | top for m in odd] + odd + [m | top for m in even] + even


def relative_cols(x, me, order):
    n = len(order)
    cols = x.shape[-1] // n
    blocks = [x[..., q * cols:(q + 1) * cols] for q in range(n)]
    bit = 1
    while bit < n:
        take = (me // bit) % 2 == 1
        blocks = [jnp.where(take, blocks[q ^ bit], blocks[q]) for q in range(n)]
        bit *= 2
    return [blocks[m] for m in order]


def gather_parts(parts, bits):
    far = bits[:-1]
    out = []
    early = None
    for turn, part in enumerate(parts):
        axes = list(range(len(far)))
        axes = axes[turn % 2:] + axes[:turn % 2]
        planes = part.shape[0]
        part = part.reshape((planes,) + (1,) * len(bits) + part.shape[1:])
        for at in axes:
            got = swap(part, "expert", far[at])
            early = got if early is None else early
            part = jnp.concatenate([part, got], axis=at + 2)
        part = jnp.concatenate([part, swap(part, "expert", bits[-1])], axis=1)
        out.append(part.reshape(-1, part.shape[-1]))
    return out, early


def plus(a, b):
    return (a.astype(F32) + b.astype(F32)).astype(BF16)


def core_sum(x, bits):
    x = x.reshape((2, x.shape[0] // 2) + x.shape[1:])
    return plus(x[0], swap(x[1], "expert", bits[-1]))


def far_sum(x, bits):
    total = x[0].astype(F32)
    for m in range(1, x.shape[0]):
        total = total + swap(x[m], "expert", m * 2).astype(F32)
    return total.astype(BF16)


def load_weights(place, weight, buffer, sems, blocks, half_index):
    slots, width, hidden = weight.shape
    rows, half = width // blocks, hidden // 2
    copies = []
    for i in range(blocks):
        for s in range(slots):
            copies.append(
                pltpu.make_async_copy(
                    weight.at[
                        s,
                        pl.ds(pl.multiple_of(place[i] * rows, rows), rows),
                        pl.ds(pl.multiple_of(half_index * half, half), half),
                    ],
                    buffer.at[pl.ds(i * rows, rows), pl.ds(s * half, half)],
                    sems.at[i * slots + s],
                )
            )
    for copy in copies:
        copy.start()
    for copy in copies:
        copy.wait()


def hidden_kernel(blocks, experts, place, first, second, weight, *rest):
    act, slope, buffer, sems = rest[-4:]
    slots = weight.shape[0]
    split = first.shape[1]
    width = weight.shape[1]

    @pl.when(pl.program_id(0) == 0)
    def _():
        load_weights(place, weight, buffer, sems, blocks, place[blocks])

    pre = jnp.dot(first[...], buffer[:split], preferred_element_type=F32) + jnp.dot(
        second[:, :width - split], buffer[split:], preferred_element_type=F32
    )
    coefs = second[:, width - split:].astype(F32)
    lane = lax.broadcasted_iota(jnp.int32, coefs.shape, 1)
    half = pre.shape[1] // slots
    for s in range(slots):
        wanted = place[blocks + 1] * slots + s
        named = (lane == wanted) | (lane == wanted + experts)
        coef = jnp.sum(jnp.where(named, coefs, 0.0), axis=1, keepdims=True)
        one = pre[:, s * half:(s + 1) * half]
        sigma = 1.0 / (1.0 + jnp.exp(-one))
        act[:, s * half:(s + 1) * half] = (coef * (one * sigma)).astype(BF16)
        slope[:, s * half:(s + 1) * half] = (coef * (sigma * (1.0 + one * (1.0 - sigma)))).astype(BF16)


def hidden_product(place, parts, weight, experts, total_rows, at_row, filled=None, given=(), tile=256):
    first, second = parts
    slots, width, hidden = weight.shape
    blocks = place.shape[0] - 2
    cols = slots * hidden // 2
    rows = first.shape[0]
    skip = at_row // tile
    shape = jax.ShapeDtypeStruct((total_rows, cols), BF16)
    any_space = pl.BlockSpec(memory_space=pl.ANY)
    held = () if filled is None else tuple(filled)
    return pl.pallas_call(
        functools.partial(hidden_kernel, blocks, experts),
        out_shape=[shape, shape],
        grid_spec=pltpu.PrefetchScalarGridSpec(
            num_scalar_prefetch=1,
            grid=(rows // tile,),
            in_specs=[
                pl.BlockSpec((tile, first.shape[1]), lambda i, p: (i, 0)),
                pl.BlockSpec((tile, second.shape[1]), lambda i, p: (i, 0)),
                any_space,
            ]
            + [any_space] * (len(held) + len(given)),
            out_specs=[pl.BlockSpec((tile, cols), lambda i, p: (i + skip, 0))] * 2,
            scratch_shapes=[
                pltpu.VMEM((width, cols), BF16),
                pltpu.SemaphoreType.DMA((blocks * slots,)),
            ],
        ),
        input_output_aliases={4: 0, 5: 1} if held else {},
        compiler_params=pltpu.CompilerParams(vmem_limit_bytes=16 * MIB),
        cost_estimate=pl.CostEstimate(
            flops=2 * rows * width * cols,
            bytes_accessed=2 * (rows * width + width * cols + 2 * rows * cols),
            transcendentals=rows * cols,
        ),
        name="hidden_product",
    )(place, first, second, weight, *held, *given)


def back_kernel(blocks, count, place, *refs):
    parts, weight, slope = refs[:count], refs[count], refs[count + 1]
    out, buffer, sems = refs[-3:]

    @pl.when(pl.program_id(0) == 0)
    def _():
        load_weights(place, weight, buffer, sems, blocks, place[blocks])

    total = None
    at = 0
    for part in parts:
        depth = part.shape[1]
        term = jnp.dot(part[...], buffer[at:at + depth], preferred_element_type=F32)
        total = term if total is None else total + term
        at += depth
    out[...] = (total * slope[...].astype(F32)).astype(BF16)


def back_product(place, parts, weight, slope, given=(), tile=256):
    slots, width, hidden = weight.shape
    blocks = place.shape[0] - 2
    cols = slots * hidden // 2
    rows = slope.shape[0]
    return pl.pallas_call(
        functools.partial(back_kernel, blocks, len(parts)),
        out_shape=jax.ShapeDtypeStruct((rows, cols), BF16),
        grid_spec=pltpu.PrefetchScalarGridSpec(
            num_scalar_prefetch=1,
            grid=(rows // tile,),
            in_specs=[pl.BlockSpec((tile, part.shape[1]), lambda i, p: (i, 0)) for part in parts]
            + [pl.BlockSpec(memory_space=pl.ANY), pl.BlockSpec((tile, cols), lambda i, p: (i, 0))]
            + [pl.BlockSpec(memory_space=pl.ANY)] * len(given),
            out_specs=pl.BlockSpec((tile, cols), lambda i, p: (i, 0)),
            scratch_shapes=[
                pltpu.VMEM((width, cols), BF16),
                pltpu.SemaphoreType.DMA((blocks * slots,)),
            ],
        ),
        compiler_params=pltpu.CompilerParams(vmem_limit_bytes=16 * MIB),
        cost_estimate=pl.CostEstimate(
            flops=2 * rows * width * cols,
            bytes_accessed=2 * (rows * width + width * cols + 2 * rows * cols),
            transcendentals=0,
        ),
        name="back_product",
    )(place, *parts, weight, slope, *given)


def out_kernel(place, own, rest, weight, out, buffer, sems):
    slots, _, hidden = weight.shape
    half = hidden // 2
    rows = out.shape[0]

    @pl.when(pl.program_id(0) == 0)
    def _():
        copies = []
        for s in range(slots):
            for k, (source, index) in enumerate(((own, place[0]), (rest, 1 - place[0]))):
                copies.append(
                    pltpu.make_async_copy(
                        source.at[pl.ds(0, rows), pl.ds(s * half, half)],
                        buffer.at[s, :, pl.ds(pl.multiple_of(index * half, half), half)],
                        sems.at[2 * s + k],
                    )
                )
        for copy in copies:
            copy.start()
        for copy in copies:
            copy.wait()

    total = None
    for s in range(slots):
        term = lax.dot_general(
            buffer[s], weight[s], (((1,), (1,)), ((), ())), preferred_element_type=F32
        )
        total = term if total is None else total + term
    out[...] = total.astype(BF16)


def out_product(half_index, own, rest, weight, tile=256):
    slots, width, hidden = weight.shape
    rows = rest.shape[0]
    return pl.pallas_call(
        out_kernel,
        out_shape=jax.ShapeDtypeStruct((rows, width), BF16),
        grid_spec=pltpu.PrefetchScalarGridSpec(
            num_scalar_prefetch=1,
            grid=(width // tile,),
            in_specs=[
                pl.BlockSpec(memory_space=pl.ANY),
                pl.BlockSpec(memory_space=pl.ANY),
                pl.BlockSpec((slots, tile, hidden), lambda i, p: (0, i, 0)),
            ],
            out_specs=pl.BlockSpec((rows, tile), lambda i, p: (0, i)),
            scratch_shapes=[
                pltpu.VMEM((slots, rows, hidden), BF16),
                pltpu.SemaphoreType.DMA((2 * slots,)),
            ],
        ),
        compiler_params=pltpu.CompilerParams(vmem_limit_bytes=16 * MIB),
        cost_estimate=pl.CostEstimate(
            flops=2 * rows * width * slots * hidden,
            bytes_accessed=2 * (rows * width + width * slots * hidden + rows * slots * hidden),
            transcendentals=0,
        ),
        name="out_product",
    )(half_index, own, rest, weight)


def outer(left, right):
    return lax.dot_general(left, right, (((0,), (0,)), ((), ())), preferred_element_type=F32)


def body(tokens, expert_ids, combine_weight, partner, w_up, w_down, out_grad):
    owners = lax.axis_size("expert")
    groups = lax.axis_size("dp")
    me_g = lax.axis_index("dp")
    me_j = lax.axis_index("expert")
    tok_dev, chosen = expert_ids.shape
    width = tokens.shape[1]
    slots = w_up.shape[1]
    hidden = w_up.shape[2]
    half = hidden // 2
    experts = slots * owners
    rows = width // groups
    top = groups // 2
    upper = me_g // top == 1
    upper_index = (me_g // top).astype(jnp.int32)
    order = block_order(groups)
    bits = [owners >> (i + 1) for i in range(owners.bit_length() - 1)]
    plane = owners * tok_dev
    scale = 1.0 / tok_dev

    named = expert_ids[:, :, None] == jnp.arange(experts, dtype=jnp.int32)[None, None, :]
    coef = jnp.sum(jnp.where(named, combine_weight[:, :, None], 0.0), axis=1)
    coef_hi = lax.reduce_precision(coef, 8, 7)
    coef_lo = coef - coef_hi
    lanes = -(-2 * experts // 128) * 128
    extra = jnp.pad(
        jnp.concatenate([coef_hi, coef_lo], axis=1), ((0, 0), (0, lanes - 2 * experts))
    ).astype(BF16)

    quarter = groups // 4

    def quarters(x):
        blocks = relative_cols(x, me_g, order)
        return [jnp.concatenate(blocks[i * quarter:(i + 1) * quarter], axis=-1) for i in range(4)]

    token_quarters = quarters(tokens)
    own_first = jnp.concatenate(token_quarters[:2], axis=1)[None]
    own_second = jnp.concatenate(token_quarters[2:] + [extra], axis=1)[None]
    x_own, early = gather_parts([own_first, own_second], bits)
    other_first = swap(own_first, "dp", top)
    other_second = swap(own_second, "dp", top)
    x_other, early = gather_parts([after(other_first, early), after(other_second, early)], bits)

    own_grads = quarters(out_grad)
    got_send = swap(after(jnp.concatenate(own_grads[:2], axis=1), other_first), "dp", top)
    got_keep = swap(after(jnp.concatenate(own_grads[2:], axis=1), got_send), "dp", top)

    def pair(own, got):
        cols = own[0].shape[1]
        return [jnp.stack([own[i], got[:, (1 - i) * cols:(2 - i) * cols]], axis=0) for i in range(2)]

    g_send, early = gather_parts([after(one, early) for one in pair(own_grads[:2], got_send)], bits)
    g_keep, _ = gather_parts([after(one, early) for one in pair(own_grads[2:], got_keep)], bits)
    g_parts = g_send + g_keep

    up = jnp.swapaxes(w_up, 0, 1)
    down = jnp.swapaxes(w_down, 0, 1)

    offsets = jnp.stack([me_g ^ m for m in order]).astype(jnp.int32)
    me_word = me_j.astype(jnp.int32)

    def place_of(half_index, change=0):
        return jnp.concatenate([offsets ^ change, half_index[None], me_word[None]])

    place = place_of(upper_index)
    both = hidden_product(place, x_own, up, experts, 2 * plane, 0)
    act, slope = hidden_product(place_of(upper_index, top), x_other, up, experts, 2 * plane, plane, both)

    def down_block(m):
        part, col = divmod(order.index(m) * rows, width // 4)
        return outer(g_parts[part][:, col:col + rows], act) * scale

    def cut(x, pieces):
        wide = x.shape[1] // pieces
        return [x[:, i * wide:(i + 1) * wide] for i in range(pieces)]

    def sent_blocks(block_of, pieces):
        return {m: cut(block_of(m).astype(BF16), pieces) for m in order if m & (top - 1)}

    def reduced(sends, block_of, pieces, ready):
        kept = {m: cut(block_of(m), pieces) for m in (top, 0)}
        for i in range(pieces):
            have = {m: sends[m][i] for m in sends}
            for m in sends:
                bit = m & -m
                piece = swap(have[m], "dp", bit)
                to = m ^ bit
                if to in kept:
                    kept[to][i] = kept[to][i] + piece.astype(F32)
                else:
                    have[to] = plus(have[to], piece)
        leaving = [x.astype(BF16) for x in kept[top]]
        own = [x.astype(BF16) for x in kept[0]]
        return own, [ready(x) for x in leaving]

    def whole(own, leaving, pieces):
        got = [swap(x, "dp", top) for x in leaving]
        if pieces == 1:
            own, got = cut(own[0], slots), cut(got[0], slots)
        return [
            jnp.where(upper, jnp.concatenate([b, a], axis=1), jnp.concatenate([a, b], axis=1))
            for a, b in zip(own, got)
        ]

    def relocated(per_slot):
        first = per_slot[0].reshape(owners, rows // owners, hidden)
        spread = lax.all_to_all(first, "expert", split_axis=0, concat_axis=0, tiled=True)
        moved = lax.all_to_all(spread[partner], "expert", split_axis=0, concat_axis=0, tiled=True)
        return jnp.stack([moved.reshape(rows, hidden)] + per_slot[1:], axis=1)

    down_sends = sent_blocks(down_block, 1)
    pre = back_product(place, g_parts, down, slope, given=[x[0] for x in down_sends.values()])

    def up_block(m):
        part, col = divmod(order.index(m) * rows, width // 2)
        other_part, other_col = divmod(order.index(m ^ top) * rows, width // 2)
        return (
            outer(x_own[part][:, col:col + rows], pre[:plane])
            + outer(x_other[other_part][:, other_col:other_col + rows], pre[plane:])
        ) * scale

    up_sends = sent_blocks(up_block, slots)
    down_own, down_leaving = reduced(down_sends, down_block, 1, lambda x: x)

    rest_place = place_of(1 - upper_index)
    act_rest, slope_rest = hidden_product(
        rest_place, x_own, up, experts, plane, 0, given=down_leaving + [x[-1] for x in up_sends.values()]
    )
    part_out = out_product(upper_index[None], act, act_rest, down)
    out_core = core_sum(part_out.reshape(owners, tok_dev, width), bits)
    pre_rest = back_product(rest_place, g_parts, down, slope_rest)
    part_in = out_product(upper_index[None], pre, pre_rest, up)
    in_core = core_sum(part_in.reshape(owners, tok_dev, width), bits)

    up_own, up_leaving = reduced(up_sends, up_block, slots, lambda x: after(x, out_core))
    up_leaving = up_leaving[:-1] + [after(up_leaving[-1], in_core)]
    grad_down = relocated(whole(down_own, down_leaving, 1))
    grad_up = relocated(whole(up_own, up_leaving, slots))
    output = far_sum(out_core, bits)
    input_grad = far_sum(in_core, bits)
    return (output, input_grad, grad_up, grad_down)


def solution(mesh):
    return jax.shard_map(
        body,
        mesh=mesh,
        in_specs=(
            P(("dp", "expert"), None),
            P(("dp", "expert"), None),
            P(("dp", "expert"), None),
            P(),
            P(None, "expert", None),
            P(None, "expert", None),
            P(("dp", "expert"), None),
        ),
        out_specs=(
            P(("dp", "expert"), None),
            P(("dp", "expert"), None),
            P("dp", "expert", None),
            P("dp", "expert", None),
        ),
        check_vma=False,
    )
```
